32 devices in a mesh: member: 2 (over x), col: 16 (over z, y, core).
Axes of the slice: x: 2, y: 2, z: 4, core: 2. Of those that a mesh axis runs over, the one named last changes fastest.
Arguments:
- air_prognostic_variables: float32 [3, 72, 65536], P(None, None, ('member', 'col')), parts along dimension 2, may hold values from -6 to 6
- air_observed_warmth: float32 [65536], P(('member', 'col')), parts along dimension 0, may hold values from -6 to 6
- air_adjacency_list: int32 [4, 32768], P(None, 'col'), may hold values from 0 to 2303, as said below
- air_diffusivity_profile: float32 [72, 72], replicated, may hold values from 0 to 0.0075
- marine_prognostic_variables: float32 [3, 80, 32768], P(None, None, ('member', 'col')), parts along dimension 2, may hold values from -6 to 6
- sealevel_elevation: float32 [32768], P(('member', 'col')), parts along dimension 0, may hold values from -6 to 6
- marine_adjacency_lists: int32 [6, 16384], P(None, 'col'), may hold values from 0 to 1279, as said below
- marine_face_factors: float32 [6, 16384], P(None, 'col'), may hold values from 0.02 to 0.14
- marine_indicator: int32 [16384], P('col'), may hold values 0 or 1
- marine_diffusivity_profile: float32 [80, 80], replicated, may hold values from 0 to 0.0075
- interpolation_donor_group: int32 [128, 4], replicated, may hold values from 0 to 255, as said below
- interpolation_factor_array: float32 [128, 4, 128, 128], P('col'), may hold values from 0.0005 to 0.005
Outputs:
- atm_out: float32 [3, 72, 65536], P(None, None, ('member', 'col')), parts along dimension 2
- ocn_out: float32 [3, 80, 32768], P(None, None, ('member', 'col')), parts along dimension 2
- ssh_out: float32 [32768], P(('member', 'col')), parts along dimension 0
- skin_upon_air_grid: float32 [3, 65536], P(None, ('member', 'col')), parts along dimension 1
The draws below stay inside these ranges and needn't reach their ends.
There are 2 independent parts, one for each index of `member`. The reference program is written for one: setup_inputs(seed, part) draws one part's arguments, and reference() takes and returns one part's arrays. A program takes and returns all parts, laid end to end along the dimension named above; an argument that names none is the same for every part. Nothing has to cross between parts.
Inputs may be any that keep to these rules, and one draw needn't show every extreme that they name: `air_adjacency_list`: entry [k, c] names the neighbour g_a(k, c) of the steps; every neighbour lies within 128 columns of c. `marine_adjacency_lists`: entry [k, c] names the neighbour g_o(k, c) of the steps; every neighbour lies within 128 cells of c. `interpolation_donor_group`: ocean block B lies on col index B // 8, atmosphere block A on index A // 16. Of the 32 references of the ocean blocks of one index, exactly 16 name atmosphere blocks of the same index; each other one names a block of the index one below or one above, wrapping around.
All inputs are finite; a program needn't handle non-finite values. No bound on the sum of `marine_indicator` on one device may be relied on, other than what follows from the above.
Results may differ from the reference program's by a relative error of at most 0.0001.
Values sent between devices are 32-bit elements; how exact they have to be, the bound alone decides.
A program may use at most 64 MiB of HBM per device.

```python
import math
import jax
import jax.numpy as jnp
from jax import lax

LEV_A = 72
LEV_O = 80
ATM_DEV = 2048
OC_DEV = 1024
NBR_A = 4
RIM_A = 128
SUB_A = 4
NBR_O = 6
RIM_O = 128
BT_SUB = 10
BC_SUB = 2
NFLUX = 4
NBACK = 4
REFS = 4
BLOCK = 128
ABLK_DEV = 16
OBLK_DEV = 8
CAP = 16
AIR_PROFILES = 32768
NO = 16384
NABLK = 256
NOBLK = 128


def near_links(key, count, total, per_block, reach):
    offset = jax.random.randint(key, (count, total), -reach, reach + 1)
    inside = jnp.arange(total, dtype=jnp.int32) % per_block
    row_ids = jnp.arange(count, dtype=jnp.int32)[:, None]
    offset = jnp.where((row_ids == 0) & (inside[None, :] == 0), -reach, offset)
    offset = jnp.where((row_ids == count - 1) & (inside[None, :] == per_block - 1), reach, offset)
    return (reach + inside[None, :] + offset).astype(jnp.int32)


def draw_air_adjacency_list(key, part):
    key = jax.random.fold_in(key, 11)
    return near_links(key, NBR_A, AIR_PROFILES, ATM_DEV, RIM_A)


def draw_marine_adjacency_lists(key, part):
    key = jax.random.fold_in(key, 12)
    return near_links(key, NBR_O, NO, OC_DEV, RIM_O)


def draw_interpolation_donor_group(key, part):
    key = jax.random.fold_in(key, 13)
    devices = NOBLK // OBLK_DEV
    count = OBLK_DEV * REFS
    key_side, key_block, key_order = jax.random.split(key, 3)
    slot_ids = jnp.broadcast_to(jnp.arange(count, dtype=jnp.int32)[None, :], (devices, count))
    side = 2 * jax.random.randint(key_side, (devices, count), 0, 2) - 1
    offset = jnp.where(slot_ids < CAP, 0, side)
    local_block = jax.random.randint(key_block, (devices, count), 0, ABLK_DEV)
    local_block = jnp.where(slot_ids == 0, ABLK_DEV - 1, jnp.where(slot_ids == 1, 0, local_block))
    scores = jax.random.randint(key_order, (devices, count), 0, 1 << 20) * count + slot_ids
    order = jnp.argsort(scores, axis=1)
    offset = jnp.take_along_axis(offset, order, axis=1)
    local_block = jnp.take_along_axis(local_block, order, axis=1)
    device_ids = jnp.arange(devices, dtype=jnp.int32)[:, None]
    blocks = (device_ids + offset) % devices * ABLK_DEV + local_block
    return blocks.reshape(NOBLK, REFS).astype(jnp.int32)


def place_ends(array, stream_key, low, high):
    shape = array.shape
    spot = [jax.random.randint(jax.random.fold_in(stream_key, axis), (), 0, shape[axis]) for axis in range(len(shape))]
    array = array.at[tuple(spot)].set(low)
    longest = shape.index(max(shape))
    spot[longest] = (spot[longest] + 1) % shape[longest]
    return array.at[tuple(spot)].set(high)


def steps_of(stream_key, shape, cuts, low, largest):
    loudness = 1.0
    for position, blocks in cuts:
        heights = jax.random.uniform(jax.random.fold_in(jax.random.fold_in(stream_key, 6), position), (blocks,), jnp.float32, low / len(cuts), largest / len(cuts))
        loudness = loudness * jnp.repeat(jnp.exp(heights), shape[position] // blocks).reshape((-1,) + (1,) * (len(shape) - 1 - position))
    return loudness


def noise(key, dims, scale, most, cuts=(), held_as=jnp.bfloat16):
    gain = steps_of(key, dims, cuts, -0.22, 0.18) if cuts else 1.0
    values = jax.random.normal(key, dims, jnp.float32) * scale * gain
    return jnp.minimum(jnp.maximum(values, -most), most).astype(held_as)


def setup_inputs(seed: int = 0, part: int = 0) -> dict:
    splits = jax.random.split(jax.random.key(seed), 13)
    part_splits = jax.random.split(jax.random.fold_in(splits[12], part), 13)
    air_prognostic_variables = noise(part_splits[0], (3, LEV_A, AIR_PROFILES), 1.0, 6.0, ((2, 16),), jnp.float32)
    air_observed_warmth = noise(part_splits[1], (AIR_PROFILES,), 1.0, 6.0, ((0, 16),), jnp.float32)
    air_adjacency_list = draw_air_adjacency_list(jax.random.fold_in(splits[12], 71), part)
    air_diffusivity_profile = jnp.clip(jax.random.uniform(splits[3], (LEV_A, LEV_A), jnp.float32, 0.0, 0.0075), 0.0, 0.0075)
    marine_prognostic_variables = noise(part_splits[4], (3, LEV_O, NO), 1.0, 6.0, ((2, 16),), jnp.float32)
    sealevel_elevation = noise(part_splits[5], (NO,), 1.0, 6.0, ((0, 16),), jnp.float32)
    marine_adjacency_lists = draw_marine_adjacency_lists(jax.random.fold_in(splits[12], 71), part)
    marine_face_factors = jnp.clip(0.02 + 0.12000000104308128 * jax.random.uniform(splits[7], (NBR_O, NO), jnp.float32) ** steps_of(splits[7], (NBR_O, NO), ((1, 16),), -0.2, 0.2), 0.02, 0.14)
    marine_indicator = place_ends((jax.random.randint(splits[8], (NO,), 0, 10) < 7).astype(jnp.int32), jax.random.fold_in(splits[8], 1), 0, 1)
    marine_diffusivity_profile = jnp.clip(jax.random.uniform(splits[9], (LEV_O, LEV_O), jnp.float32, 0.0, 0.0075), 0.0, 0.0075)
    interpolation_donor_group = draw_interpolation_donor_group(jax.random.fold_in(splits[12], 71), part)
    interpolation_factor_array = jnp.clip(jnp.exp(math.log(0.005) - 2.30258502 * jax.random.uniform(splits[11], (NOBLK, REFS, BLOCK, BLOCK), jnp.float32) ** steps_of(splits[11], (NOBLK, REFS, BLOCK, BLOCK), ((0, 16),), -0.2, 0.2)), 0.0005, 0.005)
    return {"air_prognostic_variables": air_prognostic_variables, "air_observed_warmth": air_observed_warmth, "air_adjacency_list": air_adjacency_list, "air_diffusivity_profile": air_diffusivity_profile, "marine_prognostic_variables": marine_prognostic_variables, "sealevel_elevation": sealevel_elevation, "marine_adjacency_lists": marine_adjacency_lists, "marine_face_factors": marine_face_factors, "marine_indicator": marine_indicator, "marine_diffusivity_profile": marine_diffusivity_profile, "interpolation_donor_group": interpolation_donor_group, "interpolation_factor_array": interpolation_factor_array}


highest = lax.Precision.HIGHEST


def skin_interface_transfers(lowermost_layer, prior_skin_warmth):
    return jnp.stack([0.5 * (lowermost_layer[0] - prior_skin_warmth), 0.3 * lowermost_layer[1] * lowermost_layer[2], 0.5 * lowermost_layer[1], 0.5 * lowermost_layer[2]])


def global_index(links, per_block, reach, total):
    cell_ids = jnp.arange(total, dtype=jnp.int32)
    first_cell = (cell_ids // per_block) * per_block
    return ((first_cell[None, :] + links - reach) % total).astype(jnp.int32)


def atm_update(extended, center, links, mixing):
    totals = jnp.zeros_like(center)
    for neighbour in range(links.shape[0]):
        totals = totals + (jnp.take(extended, links[neighbour], axis=-1) - center)
    blended = center + 0.22 * totals
    return 0.6 * blended + jnp.einsum('lm,fmc->flc', mixing, blended, precision=highest)


def ocean_spread(extended, center, links, weights):
    totals = jnp.zeros_like(center)
    for neighbour in range(links.shape[0]):
        totals = totals + weights[neighbour] * (jnp.take(extended, links[neighbour], axis=-1) - center)
    return totals


def reference(air_prognostic_variables, air_observed_warmth, air_adjacency_list, air_diffusivity_profile, marine_prognostic_variables, sealevel_elevation, marine_adjacency_lists, marine_face_factors, marine_indicator, marine_diffusivity_profile, interpolation_donor_group, interpolation_factor_array):
    lowermost_layer = air_prognostic_variables[:, LEV_A - 1, :]
    interface_transfers = skin_interface_transfers(lowermost_layer, air_observed_warmth)
    atm_links = global_index(air_adjacency_list, ATM_DEV, RIM_A, AIR_PROFILES)
    atm_now = air_prognostic_variables
    for substep in range(SUB_A):
        atm_now = atm_update(atm_now, atm_now, atm_links, air_diffusivity_profile)
    flux_blocks = interface_transfers.reshape(NFLUX, NABLK, BLOCK)
    picked = jnp.take(flux_blocks, interpolation_donor_group.reshape(-1), axis=1).reshape(NFLUX, NOBLK, REFS, BLOCK)
    ocean_flux = jnp.einsum('brao,fbra->fbo', interpolation_factor_array, picked, precision=highest).reshape(NFLUX, NO)
    ocn_links = global_index(marine_adjacency_lists, OC_DEV, RIM_O, NO)
    ocean_mask = marine_indicator.astype(jnp.float32)
    column_state = marine_prognostic_variables * ocean_mask
    surface_height = sealevel_elevation * ocean_mask
    freshwater = 0.1 * ocean_flux[1]
    forcing = 0.2 * jnp.stack([ocean_flux[0], ocean_flux[2], ocean_flux[3]]) * ocean_mask
    for baroclinic in range(BC_SUB):
        for barotropic in range(BT_SUB):
            surface_height = ocean_mask * (surface_height + ocean_spread(surface_height, surface_height, ocn_links, marine_face_factors) + freshwater)
        blended = column_state + ocean_spread(column_state, column_state, ocn_links, marine_face_factors)
        column_state = ocean_mask * (0.6 * blended + jnp.einsum('lm,fmc->flc', marine_diffusivity_profile, blended, precision=highest))
        column_state = column_state.at[:, 0, :].add(forcing)
    surface = jnp.stack([column_state[0, 0], column_state[1, 0], column_state[2, 0], ocean_mask]).reshape(NBACK, NOBLK, BLOCK)
    pieces = jnp.einsum('brao,fbo->fbra', interpolation_factor_array, surface, precision=highest).reshape(NBACK, NOBLK * REFS, BLOCK)
    reply_skin_values = jnp.zeros((NBACK, NABLK, BLOCK), jnp.float32).at[:, interpolation_donor_group.reshape(-1)].add(pieces).reshape(NBACK, AIR_PROFILES)
    marine_share = 1.0 + reply_skin_values[3]
    skin_upon_air_grid = jnp.stack([(air_observed_warmth + reply_skin_values[0]) / marine_share, reply_skin_values[1] / marine_share, reply_skin_values[2] / marine_share])
    return atm_now, column_state, surface_height, skin_upon_air_grid
```

```python
import functools

import jax
import jax.numpy as jnp
from jax import lax
from jax.experimental import pallas as pl
from jax.experimental.pallas import tpu as pltpu
from jax.sharding import PartitionSpec as P

BLOCK = 128
SUB_A = 4
BT_SUB = 10
BC_SUB = 2
MESH = pl.DeviceIdType.MESH
F32 = jnp.float32
BF16 = jnp.bfloat16
HIGHEST = lax.Precision.HIGHEST
FAR = 3
HA = SUB_A * BLOCK
HO = BC_SUB * BLOCK


def iota(shape, dim):
    return lax.broadcasted_iota(jnp.int32, shape, dim)


def dot(a, b):
    return jnp.dot(a, b, preferred_element_type=F32)


def dot_exact(a, b):
    return jnp.dot(a, b, preferred_element_type=F32, precision=HIGHEST)


def pieces_of(x):
    hi = x.astype(BF16)
    return hi, (x - hi.astype(F32)).astype(BF16)


def level_operator(profile):
    n = profile.shape[0]
    return profile + jnp.where(iota((n, n), 0) == iota((n, n), 1), F32(0.6), F32(0.0))


def spread_columns(matrix, field, width):
    n = matrix.shape[0]
    place = (iota((n, width), 1) == iota((n, width), 0) + field * n).astype(F32)
    return dot_exact(matrix, place)


def gather_lanes(rows, lanes):
    return jnp.take_along_axis(rows, lanes, axis=1, mode="promise_in_bounds")


def main_kernel(
    n,
    air, warm, alist, mar, sea, mlist, mff, mind, mdiff, donor, weights,
    t_out, y_out, tot_out, ssh_out,
    low, centre, left, right, xc, xl, xr, lx, lleft, lright,
    wf, whi, wlo, cand, px, ofx, idx, coef, eta, forc, gath, op, fhi, flo,
    hla, hlb, xa, xb, pc, coll, rb,
    ss, rs, ls,
):
    levels_a = air.shape[1]
    levels_o = mar.shape[1]
    na = air.shape[2]
    no = mar.shape[2]
    ab = na // BLOCK
    ob = no // BLOCK
    rows_a = hla.shape[0] // 2
    rows_o = xa.shape[0] // 2
    refs = donor.shape[0]
    me = lax.axis_index("col")

    def peer(d):
        return {"col": lax.rem(me + d + n, n)}

    def remote(src, dst, i, d):
        return pltpu.make_async_remote_copy(
            src_ref=src, dst_ref=dst, send_sem=ss.at[i], recv_sem=rs.at[i],
            device_id=peer(d), device_id_type=MESH,
        )

    low_copy = pltpu.make_async_copy(air.at[:, levels_a - 8 :, :], low, ls.at[0])
    low_copy.start()
    w_copy = pltpu.make_async_copy(weights, wf, ls.at[1])
    air_copy = pltpu.make_async_copy(air, centre, ls.at[2])
    mar_copy = pltpu.make_async_copy(mar, xc, ls.at[3])
    w_copy.start()
    mar_copy.start()
    air_copy.start()
    far = [d for d in range(-FAR, FAR + 1) if d != 0]
    barrier = pltpu.get_barrier_semaphore()
    for d in far:
        pl.semaphore_signal(barrier, inc=1, device_id=peer(d), device_id_type=MESH)

    for b in range(ob):
        cols = slice(b * BLOCK, (b + 1) * BLOCK)
        px[FAR, 0:6, b, :] = mlist[:, cols].astype(F32)
        px[FAR, 6:12, b, :] = mff[:, cols]
    px[FAR, 12, :, :] = mind[...].astype(F32)
    px[FAR, 13, :, :] = sea[...]

    low_copy.wait()
    lowest = [low[f, 7:8, :] for f in range(3)]
    flux = jnp.concatenate(
        [
            0.5 * (lowest[0] - warm[...]),
            0.3 * lowest[1] * lowest[2],
            0.5 * lowest[1],
            0.5 * lowest[2],
        ],
        axis=0,
    )
    for b in range(ab):
        cand[ab + b] = flux[:, b * BLOCK : (b + 1) * BLOCK]

    pl.semaphore_wait(barrier, len(far))
    flux_sends = [
        remote(cand.at[ab : 2 * ab], cand.at[0:ab], 0, 1),
        remote(cand.at[ab : 2 * ab], cand.at[2 * ab : 3 * ab], 1, -1),
    ]
    table_sends = [remote(px.at[FAR], px.at[FAR - d], 2 + i, d) for i, d in enumerate(far)]
    list_sends = [
        remote(alist.at[:, na - HA : na], lleft, 8, 1),
        remote(alist.at[:, 0:HA], lright, 9, -1),
    ]
    mar_sends = [
        remote(mar.at[:, :, no - HO : no], xl, 10, 1),
        remote(mar.at[:, :, 0:HO], xr, 11, -1),
    ]
    air_sends = [
        remote(air.at[:, :, na - HA : na], left, 12, 1),
        remote(air.at[:, :, 0:HA], right, 13, -1),
    ]
    for c in flux_sends + table_sends + list_sends + mar_sends + air_sends:
        c.start()

    pairs = ab // 2 + SUB_A
    zero_block = jnp.zeros((BLOCK, BLOCK), BF16)

    def build_air(j, carry):
        op[j, 3 * BLOCK : 4 * BLOCK, 0:BLOCK] = zero_block
        op[j, 0:BLOCK, BLOCK : 2 * BLOCK] = zero_block
        for side in range(2):
            e = 2 * j + side
            b = lax.rem(e + ab - SUB_A, ab)
            links = lx[:, pl.ds(pl.multiple_of(e * BLOCK, BLOCK), BLOCK)] - b * BLOCK
            for part in range(3):
                ids = iota((BLOCK, BLOCK), 0) + part * BLOCK
                total = jnp.zeros((BLOCK, BLOCK), F32)
                for k in range(links.shape[0]):
                    total = total + jnp.where(links[k : k + 1, :] == ids, F32(1.0), F32(0.0))
                r = (part + side) * BLOCK
                op[j, r : r + BLOCK, side * BLOCK : (side + 1) * BLOCK] = total.astype(BF16)
        return carry

    lx[:, HA : HA + na] = alist[...]
    half = SUB_A // 2
    lax.fori_loop(half, pairs - half, build_air, 0)

    w_copy.wait()

    def split_weights(b, carry):
        hi, lo = pieces_of(wf[b])
        whi[b] = hi
        wlo[b] = lo
        return carry

    lax.fori_loop(0, ob, split_weights, 0)

    def place_of(b, r):
        ref = donor[r, me * ob + b]
        owner = ref // ab
        off = lax.rem(owner - me + n, n)
        base = jnp.where(off == 0, ab, jnp.where(off == 1, 2 * ab, 0))
        return base + lax.rem(ref, ab)

    for c in flux_sends:
        c.wait_recv()
    lane_ids = iota((8, BLOCK), 1)
    places = jnp.zeros((8, BLOCK), jnp.int32)
    for b in range(ob):
        picked = []
        for r in range(refs):
            where = place_of(b, r)
            places = jnp.where(lane_ids == b * refs + r, where, places)
            picked.append(cand[where])
        f = jnp.concatenate(picked, axis=1)
        hi = f.astype(BF16).astype(F32)
        stacked = jnp.concatenate([hi, f - hi], axis=0).astype(BF16)
        first = dot(stacked, whi[b])
        second = dot(stacked, wlo[b])
        ofx[FAR, :, b, :] = first[0:4] + first[4:8] + second[0:4]
    of_sends = [remote(ofx.at[FAR], ofx.at[FAR - d], 14 + i, d) for i, d in enumerate(far)]
    for c in of_sends:
        c.start()

    for c in table_sends:
        c.wait_recv()
    block_ids = iota((ob, BLOCK), 0) * BLOCK

    def prepare(s, carry):
        m = px[s, 12]
        total = jnp.zeros((ob, BLOCK), F32)
        for k in range(6):
            idx[s, k] = px[s, k].astype(jnp.int32) - block_ids
            w = px[s, 6 + k]
            total = total + w
            coef[s, k] = m * w
        coef[s, 6] = m * (1.0 - total)
        eta[pl.ds(pl.multiple_of(s * ob + 8, 8), ob), :] = m * px[s, 13]
        return carry

    slots = 2 * FAR + 1
    lax.fori_loop(0, slots, prepare, 0)
    eta[0:8, :] = jnp.zeros((8, BLOCK), F32)
    eta[8 + slots * ob : 16 + slots * ob, :] = jnp.zeros((8, BLOCK), F32)

    opairs = ob // 2 + BC_SUB

    def build_ocean(j, carry):
        for ref_ in (fhi, flo):
            ref_[j, 3 * BLOCK : 4 * BLOCK, 0:BLOCK] = zero_block
            ref_[j, 0:BLOCK, BLOCK : 2 * BLOCK] = zero_block
        for side in range(2):
            e = 2 * j + side + FAR * ob - BC_SUB
            s = e // ob
            b = lax.rem(e, ob)
            links = [idx[s, k, pl.ds(b, 1), :] for k in range(6)]
            values = [coef[s, k, pl.ds(b, 1), :] for k in range(7)]
            for part in range(3):
                ids = iota((BLOCK, BLOCK), 0) + part * BLOCK
                if part == 1:
                    own = iota((BLOCK, BLOCK), 0) == iota((BLOCK, BLOCK), 1)
                    total = jnp.where(own, values[6], F32(0.0))
                else:
                    total = jnp.zeros((BLOCK, BLOCK), F32)
                for k in range(6):
                    total = total + jnp.where(links[k] == ids, values[k], F32(0.0))
                r = (part + side) * BLOCK
                hi, lo = pieces_of(total)
                fhi[j, r : r + BLOCK, side * BLOCK : (side + 1) * BLOCK] = hi
                flo[j, r : r + BLOCK, side * BLOCK : (side + 1) * BLOCK] = lo
        return carry

    lax.fori_loop(0, opairs, build_ocean, 0)

    def put_ocean(value, at, buf):
        rows = value.reshape(rows_o, value.shape[2])
        hi, lo = pieces_of(rows)
        buf[0:rows_o, at : at + value.shape[2]] = hi
        buf[rows_o : 2 * rows_o, at : at + value.shape[2]] = lo

    edge_o = jnp.zeros((2 * rows_o, BLOCK), BF16)
    xa[:, 0:BLOCK] = edge_o
    xa[:, xa.shape[1] - BLOCK : xa.shape[1]] = edge_o
    mar_copy.wait()
    for b in range(ob):
        m = px[FAR, 12, b : b + 1, :]
        cols = slice(b * BLOCK, (b + 1) * BLOCK)
        put_ocean(xc[:, :, cols] * m, BLOCK + HO + b * BLOCK, xa)
    for c in mar_sends:
        c.wait_recv()
    for b in range(BC_SUB):
        cols = slice(b * BLOCK, (b + 1) * BLOCK)
        m = px[FAR - 1, 12, ob - BC_SUB + b : ob - BC_SUB + b + 1, :]
        put_ocean(xl[:, :, cols] * m, BLOCK + b * BLOCK, xa)
        m = px[FAR + 1, 12, b : b + 1, :]
        put_ocean(xr[:, :, cols] * m, BLOCK + HO + no + b * BLOCK, xa)

    def ocean_apply(j, src):
        window = src[:, pl.ds(pl.multiple_of(j * 2 * BLOCK, BLOCK), 4 * BLOCK)]
        a = dot(window, fhi[j])
        b = dot(window[0:rows_o], flo[j])
        return a[0:rows_o] + a[rows_o : 2 * rows_o] + b

    def ocean_first(j, carry):
        hi, lo = pieces_of(ocean_apply(j, xa))
        cols = pl.ds(pl.multiple_of(j * 2 * BLOCK + BLOCK, BLOCK), 2 * BLOCK)
        xb[0:rows_o, cols] = hi
        xb[rows_o : 2 * rows_o, cols] = lo
        return carry

    lax.fori_loop(0, opairs, ocean_first, 0)

    def ocean_second(j, carry):
        cols = pl.ds(pl.multiple_of((j - 1) * 2 * BLOCK, BLOCK), 2 * BLOCK)
        y_out[0:rows_o, cols] = ocean_apply(j, xb)
        return carry

    lax.fori_loop(1, opairs - 1, ocean_second, 0)

    for c in of_sends:
        c.wait_recv()

    def neighbours(prev, cur, after, s):
        total = coef[s, 6] * cur
        for k in range(6):
            at = idx[s, k]
            lanes = jnp.bitwise_and(at, BLOCK - 1)
            g0 = gather_lanes(prev, lanes)
            g1 = gather_lanes(cur, lanes)
            g2 = gather_lanes(after, lanes)
            g = jnp.where(at < BLOCK, g0, jnp.where(at < 2 * BLOCK, g1, g2))
            total = total + coef[s, k] * g
        return total

    gath[...] = jnp.zeros(gath.shape, F32)
    for i, field in enumerate((0, 2, 3)):
        for o in range(3):
            s = FAR - 1 + o
            forc[o * ob : (o + 1) * ob, :] = 0.2 * ofx[s, field] * px[s, 12]
        cur = forc[ob : 2 * ob, :]
        moved = neighbours(forc[ob - 1 : 2 * ob - 1, :], cur, forc[ob + 1 : 2 * ob + 1, :], FAR)
        gath[i] = moved
        gath[3 + i] = cur
    for b in range(ob):
        y_out[rows_o : rows_o + 16, b * BLOCK : (b + 1) * BLOCK] = gath[:, b, :]

    lo_op = level_operator(mdiff[...])
    l2 = dot_exact(lo_op[0:8], lo_op)
    width = y_out.shape[0]
    top = []
    cols = iota((1, width), 1)
    for f in range(3):
        n_l = levels_o
        place = (iota((n_l, width), 1) == iota((n_l, width), 0) + f * n_l).astype(F32)
        row = dot_exact(l2, place)[0:1]
        row = row + jnp.where(cols == rows_o + f, lo_op[0:1, 0:1], F32(0.0))
        top.append(row + jnp.where(cols == rows_o + 3 + f, F32(1.0), F32(0.0)))
    top = jnp.concatenate(top + [jnp.zeros((5, width), F32)], axis=0)
    thi = top.astype(BF16).astype(F32)
    tstack = jnp.concatenate([thi, top - thi], axis=0).astype(BF16)
    nt = (((1,), (1,)), ((), ()))
    for b in range(ob):
        yhi, ylo = pieces_of(y_out[:, b * BLOCK : (b + 1) * BLOCK])
        first = dot(tstack, yhi)
        second = dot(tstack, ylo)
        surf = first[0:8] + first[8:16] + second[0:8]
        row_ids = iota((8, BLOCK), 0)
        surf = jnp.where(row_ids == 3, px[FAR, 12, b : b + 1, :], surf)
        shi = surf.astype(BF16).astype(F32)
        sstack = jnp.concatenate([shi, surf - shi], axis=0).astype(BF16)
        first = lax.dot_general(sstack, whi[b], nt, preferred_element_type=F32)
        second = lax.dot_general(sstack, wlo[b], nt, preferred_element_type=F32)
        piece = first[0:8] + first[8:16] + second[0:8]
        for r in range(refs):
            pc[:, b * refs + r, :] = piece[0:4, r * BLOCK : (r + 1) * BLOCK]
    count = ob * refs
    hits = (iota((3 * ab, count), 0) == places[0:1, 0:count]).astype(F32)
    for f in range(4):
        coll[f] = dot_exact(hits, pc[f])
    back_sends = [
        remote(coll.at[:, 2 * ab : 3 * ab, :], rb.at[0], 20, 1),
        remote(coll.at[:, 0:ab, :], rb.at[1], 21, -1),
    ]
    for c in back_sends:
        c.start()

    for s in range(slots):
        coef[s, 7] = 0.1 * ofx[s, 1] * px[s, 12]

    def barotropic(reach):
        def step(i, carry):
            fresh = []
            for s in range(FAR - reach, FAR + reach + 1):
                r = 8 + s * ob
                fresh.append(
                    coef[s, 7]
                    + neighbours(
                        eta[r - 1 : r - 1 + ob, :], eta[r : r + ob, :], eta[r + 1 : r + 1 + ob, :], s
                    )
                )
            for s, value in zip(range(FAR - reach, FAR + reach + 1), fresh):
                eta[8 + s * ob : 8 + (s + 1) * ob, :] = value
            return carry

        return step

    steps = BT_SUB * BC_SUB
    left_over = steps
    for reach in range(FAR, -1, -1):
        stop = max((reach - 1) * ob, -1) if reach else -1
        todo = left_over - 1 - stop
        if reach == FAR:
            todo = left_over - 1 - stop
        lax.fori_loop(0, todo, barotropic(reach), 0)
        left_over -= todo
    ssh_out[...] = eta[8 + FAR * ob : 8 + (FAR + 1) * ob, :]

    pad = jnp.zeros((rows_a - 3 * levels_a, 2 * BLOCK), F32)

    def put_air(value, at, buf):
        rows = jnp.concatenate([value.reshape(3 * levels_a, 2 * BLOCK), pad], axis=0)
        hi, lo = pieces_of(rows)
        buf[0:rows_a, at] = hi
        buf[rows_a : 2 * rows_a, at] = lo

    edge_a = jnp.zeros((2 * rows_a, BLOCK), BF16)
    for buf in (hla, hlb):
        buf[:, 0:BLOCK] = edge_a
        buf[:, buf.shape[1] - BLOCK : buf.shape[1]] = edge_a
    air_copy.wait()

    def fill(j, carry):
        cols = pl.ds(pl.multiple_of(j * 2 * BLOCK, BLOCK), 2 * BLOCK)
        put_air(
            centre[:, :, cols],
            pl.ds(pl.multiple_of(j * 2 * BLOCK + BLOCK + HA, BLOCK), 2 * BLOCK),
            hla,
        )
        return carry

    lax.fori_loop(0, ab // 2, fill, 0)
    for c in list_sends + air_sends:
        c.wait_recv()
    lx[:, 0:HA] = lleft[...]
    lx[:, HA + na : 2 * HA + na] = lright[...]
    lax.fori_loop(0, half, build_air, 0)
    lax.fori_loop(pairs - half, pairs, build_air, 0)
    for j in range(half):
        cols = slice(j * 2 * BLOCK, (j + 1) * 2 * BLOCK)
        base = BLOCK + j * 2 * BLOCK
        put_air(left[:, :, cols], slice(base, base + 2 * BLOCK), hla)
        base = base + HA + na
        put_air(right[:, :, cols], slice(base, base + 2 * BLOCK), hla)

    def air_apply(j, src):
        window = src[:, pl.ds(pl.multiple_of(j * 2 * BLOCK, BLOCK), 4 * BLOCK)]
        r = dot(window, op[j])
        own = src[:, pl.ds(pl.multiple_of(j * 2 * BLOCK + BLOCK, BLOCK), 2 * BLOCK)].astype(F32)
        own = own[0:rows_a] + own[rows_a : 2 * rows_a]
        gain = 1.0 - 0.22 * alist.shape[0]
        return gain * own + 0.22 * (r[0:rows_a] + r[rows_a : 2 * rows_a])

    def air_step(src, dst):
        def step(j, carry):
            hi, lo = pieces_of(air_apply(j, src))
            cols = pl.ds(pl.multiple_of(j * 2 * BLOCK + BLOCK, BLOCK), 2 * BLOCK)
            dst[0:rows_a, cols] = hi
            dst[rows_a : 2 * rows_a, cols] = lo
            return carry

        return step

    lax.fori_loop(0, pairs, air_step(hla, hlb), 0)
    lax.fori_loop(1, pairs - 1, air_step(hlb, hla), 0)
    lax.fori_loop(1, pairs - 1, air_step(hla, hlb), 0)

    def air_last(j, carry):
        cols = pl.ds(pl.multiple_of((j - half) * 2 * BLOCK, BLOCK), 2 * BLOCK)
        t_out[:, cols] = air_apply(j, hlb)
        return carry

    lax.fori_loop(half, pairs - half, air_last, 0)

    for c in back_sends:
        c.wait_recv()
    tot_out[...] = coll[:, ab : 2 * ab, :] + rb[0] + rb[1]
    for c in flux_sends + table_sends + list_sends + mar_sends + air_sends + of_sends + back_sends:
        c.wait_send()


def last_kernel(t, y, tot, ssh, warm, adiff, mdiff, a_out, o_out, skin, ssh_out, mix_a, mix_o):
    rows_a = t.shape[0]
    rows_o = y.shape[0]
    la = adiff.shape[0]
    lo = mdiff.shape[0]
    one = level_operator(adiff[...])
    two = dot_exact(one, one)
    four = dot_exact(two, two)
    oc = level_operator(mdiff[...])
    oc2 = dot_exact(oc, oc)
    at = iota((lo, rows_o), 1)
    level = iota((lo, rows_o), 0)
    for f in range(3):
        m = spread_columns(four, f, rows_a)
        mix_a[f * la : (f + 1) * la, :] = m
        m = spread_columns(oc2, f, rows_o)
        m = m + jnp.where(at == 3 * lo + f, oc[:, 0:1], F32(0.0))
        m = m + jnp.where((at == 3 * lo + 3 + f) & (level == 0), F32(1.0), F32(0.0))
        mix_o[f * lo : (f + 1) * lo, :] = m

    def mix(src, mixer, out, levels):
        mhi, mlo = pieces_of(mixer[...])

        def step(j, carry):
            cols = pl.ds(pl.multiple_of(j * 2 * BLOCK, BLOCK), 2 * BLOCK)
            hi, lo_ = pieces_of(src[:, cols])
            r = dot(mhi, hi) + dot(mlo, hi) + dot(mhi, lo_)
            out[:, :, cols] = r.reshape(3, levels, 2 * BLOCK)
            return carry

        lax.fori_loop(0, src.shape[1] // (2 * BLOCK), step, 0)

    mix(t, mix_a, a_out, la)
    mix(y, mix_o, o_out, lo)
    share = 1.0 + tot[3]
    parts = [(warm[...] + tot[0]) / share, tot[1] / share, tot[2] / share]
    for f in range(3):
        for b in range(tot.shape[1]):
            skin[f : f + 1, b * BLOCK : (b + 1) * BLOCK] = parts[f][b : b + 1, :]
    ssh_out[...] = ssh[...]


def body(
    air, warm, alist, adiff, mar, sea, mlist, mff, mind, mdiff, donor, weights
):
    n = lax.axis_size("col")
    na = air.shape[2]
    no = mar.shape[2]
    ab = na // BLOCK
    ob = no // BLOCK
    la = air.shape[1]
    lo = mar.shape[1]
    refs = donor.shape[1]
    rows_a = -(-3 * la // 16) * 16
    rows_o = 3 * lo
    slots = 2 * FAR + 1
    pairs = ab // 2 + SUB_A
    opairs = ob // 2 + BC_SUB
    wide_a = na + 2 * HA + 2 * BLOCK
    wide_o = no + 2 * HO + 2 * BLOCK
    vmem = pl.BlockSpec(memory_space=pltpu.VMEM)
    anywhere = pl.BlockSpec(memory_space=pl.ANY)
    smem = pl.BlockSpec(memory_space=pltpu.SMEM)
    S = jax.ShapeDtypeStruct
    V = pltpu.VMEM
    t, y, tot, ssh = pl.pallas_call(
        functools.partial(main_kernel, n),
        out_shape=(
            S((rows_a, na), F32), S((rows_o + 16, no), F32), S((4, ab, BLOCK), F32), S((ob, BLOCK), F32),
        ),
        in_specs=[anywhere, vmem, vmem, anywhere, vmem, vmem, vmem, vmem, vmem, smem, anywhere],
        out_specs=(vmem, vmem, vmem, vmem),
        scratch_shapes=[
            V((3, 8, na), F32),
            V((3, la, na), F32), V((3, la, HA), F32), V((3, la, HA), F32),
            V((3, lo, no), F32), V((3, lo, HO), F32), V((3, lo, HO), F32),
            V((4, na + 2 * HA), jnp.int32), V((4, HA), jnp.int32), V((4, HA), jnp.int32),
            V((ob, refs * BLOCK, BLOCK), F32),
            V((ob, refs * BLOCK, BLOCK), BF16), V((ob, refs * BLOCK, BLOCK), BF16),
            V((3 * ab, 4, BLOCK), F32),
            V((slots, 14, ob, BLOCK), F32),
            V((slots, 4, ob, BLOCK), F32),
            V((slots, 6, ob, BLOCK), jnp.int32), V((slots, 8, ob, BLOCK), F32),
            V((slots * ob + 16, BLOCK), F32),
            V((3 * ob, BLOCK), F32),
            V((16, ob, BLOCK), F32),
            V((pairs, 4 * BLOCK, 2 * BLOCK), BF16),
            V((opairs, 4 * BLOCK, 2 * BLOCK), BF16), V((opairs, 4 * BLOCK, 2 * BLOCK), BF16),
            V((2 * rows_a, wide_a), BF16), V((2 * rows_a, wide_a), BF16),
            V((2 * rows_o, wide_o), BF16), V((2 * rows_o, wide_o), BF16),
            V((4, ob * refs, BLOCK), F32), V((4, 3 * ab, BLOCK), F32), V((2, 4, ab, BLOCK), F32),
            pltpu.SemaphoreType.DMA((22,)), pltpu.SemaphoreType.DMA((22,)), pltpu.SemaphoreType.DMA((4,)),
        ],
        compiler_params=pltpu.CompilerParams(
            collective_id=0, has_side_effects=True, vmem_limit_bytes=50 * 1024 * 1024
        ),
        name="couple",
    )(
        air, warm.reshape(1, na), alist, mar, sea.reshape(ob, BLOCK), mlist, mff,
        mind.reshape(ob, BLOCK), mdiff, donor.T, weights.reshape(ob, refs * BLOCK, BLOCK),
    )
    a_out, o_out, skin, ssh_out = pl.pallas_call(
        last_kernel,
        out_shape=(S(air.shape, F32), S(mar.shape, F32), S((3, na), F32), S((ob, BLOCK), F32)),
        in_specs=[vmem] * 7,
        out_specs=(vmem,) * 4,
        scratch_shapes=[V((3 * la, rows_a), F32), V((3 * lo, rows_o + 16), F32)],
        compiler_params=pltpu.CompilerParams(vmem_limit_bytes=50 * 1024 * 1024),
        name="mix",
    )(t, y, tot, ssh, warm.reshape(ab, BLOCK), adiff, mdiff)
    return a_out, o_out, ssh_out.reshape(no), skin


def solution(mesh):
    cells = ("member", "col")
    in_specs = (
        P(None, None, cells),
        P(cells),
        P(None, "col"),
        P(),
        P(None, None, cells),
        P(cells),
        P(None, "col"),
        P(None, "col"),
        P("col"),
        P(),
        P(),
        P("col", None, None, None),
    )
    out_specs = (P(None, None, cells), P(None, None, cells), P(cells), P(None, cells))
    return jax.shard_map(body, mesh=mesh, in_specs=in_specs, out_specs=out_specs, check_vma=False)
```

```python
import functools

import jax
import jax.numpy as jnp
from jax import lax
from jax.experimental import pallas as pl
from jax.experimental.pallas import tpu as pltpu
from jax.sharding import PartitionSpec as P

BLOCK = 128
SUB_A = 4
BT_SUB = 10
BC_SUB = 2
MESH = pl.DeviceIdType.MESH
F32 = jnp.float32
BF16 = jnp.bfloat16
HIGHEST = lax.Precision.HIGHEST
FAR = 1
ROUNDS = (7, 7, 6)
HA = SUB_A * BLOCK
HO = BC_SUB * BLOCK


def iota(shape, dim):
    return lax.broadcasted_iota(jnp.int32, shape, dim)


def dot(a, b):
    return jnp.dot(a, b, preferred_element_type=F32)


def dot_exact(a, b):
    return jnp.dot(a, b, preferred_element_type=F32, precision=HIGHEST)


def pieces_of(x):
    hi = x.astype(BF16)
    return hi, (x - hi.astype(F32)).astype(BF16)


def level_operator(profile):
    n = profile.shape[0]
    return profile + jnp.where(iota((n, n), 0) == iota((n, n), 1), F32(0.6), F32(0.0))


def spread_columns(matrix, field, width):
    n = matrix.shape[0]
    place = (iota((n, width), 1) == iota((n, width), 0) + field * n).astype(F32)
    return dot_exact(matrix, place)


def gather_lanes(rows, lanes):
    return jnp.take_along_axis(rows, lanes, axis=1, mode="promise_in_bounds")


def main_kernel(
    n,
    air, warm_in, alist_in, mar, sea_in, mlist_in, mff_in, mind_in, mdiff_in, donor_in, weights,
    t_out, y_out, tot_out, ssh_out,
    warm, alist, sea, mlist, mff, mind, mdiff, donor,
    low, centre, left, right, xc, xl, xr, lx, lleft, lright,
    wf, whi, wlo, cand, px, ofx, idx, coef, eta, forc, gath, op, fhi, flo,
    hla, hlb, xa, xb, pc, coll, rb, es, el, er,
    ss, rs, ls,
):
    levels_a = air.shape[1]
    levels_o = mar.shape[1]
    na = air.shape[2]
    no = mar.shape[2]
    ab = na // BLOCK
    ob = no // BLOCK
    rows_a = hla.shape[0] // 2
    rows_o = xa.shape[0] // 2
    refs = donor_in.shape[0]
    me = lax.axis_index("col")

    def peer(d):
        return {"col": lax.rem(me + d + n, n)}

    def remote(src, dst, i, d):
        return pltpu.make_async_remote_copy(
            src_ref=src, dst_ref=dst, send_sem=ss.at[i], recv_sem=rs.at[i],
            device_id=peer(d), device_id_type=MESH,
        )

    low_copy = pltpu.make_async_copy(air.at[:, levels_a - 8 :, :], low, ls.at[0])
    low_copy.start()
    small = [
        pltpu.make_async_copy(a, b, ls.at[4 + i])
        for i, (a, b) in enumerate(
            [
                (mlist_in, mlist), (mff_in, mff), (mind_in, mind), (sea_in, sea),
                (warm_in, warm), (alist_in, alist), (donor_in, donor), (mdiff_in, mdiff),
            ]
        )
    ]
    for c in small:
        c.start()
    w_copy = pltpu.make_async_copy(weights, wf, ls.at[1])
    air_copy = pltpu.make_async_copy(air, centre, ls.at[2])
    mar_copy = pltpu.make_async_copy(mar, xc, ls.at[3])
    w_copy.start()
    mar_copy.start()
    air_copy.start()
    far = [d for d in range(-FAR, FAR + 1) if d != 0]
    barrier = pltpu.get_barrier_semaphore()
    for d in far:
        pl.semaphore_signal(barrier, inc=1, device_id=peer(d), device_id_type=MESH)

    for c in small:
        c.wait()

    for b in range(ob):
        cols = slice(b * BLOCK, (b + 1) * BLOCK)
        px[FAR, 0:6, b, :] = mlist[:, cols].astype(F32)
        px[FAR, 6:12, b, :] = mff[:, cols]
    px[FAR, 12, :, :] = mind[...].astype(F32)
    px[FAR, 13, :, :] = sea[...]

    low_copy.wait()
    lowest = [low[f, 7:8, :] for f in range(3)]
    flux = jnp.concatenate(
        [
            0.5 * (lowest[0] - warm[...]),
            0.3 * lowest[1] * lowest[2],
            0.5 * lowest[1],
            0.5 * lowest[2],
        ],
        axis=0,
    )
    for b in range(ab):
        cand[ab + b] = flux[:, b * BLOCK : (b + 1) * BLOCK]

    pl.semaphore_wait(barrier, len(far))
    flux_sends = [
        remote(cand.at[ab : 2 * ab], cand.at[0:ab], 0, 1),
        remote(cand.at[ab : 2 * ab], cand.at[2 * ab : 3 * ab], 1, -1),
    ]
    table_sends = [remote(px.at[FAR], px.at[FAR - d], 2 + i, d) for i, d in enumerate(far)]
    list_sends = [
        remote(alist.at[:, na - HA : na], lleft, 8, 1),
        remote(alist.at[:, 0:HA], lright, 9, -1),
    ]
    mar_sends = [
        remote(mar.at[:, :, no - HO : no], xl, 10, 1),
        remote(mar.at[:, :, 0:HO], xr, 11, -1),
    ]
    air_sends = [
        remote(air.at[:, :, na - HA : na], left, 12, 1),
        remote(air.at[:, :, 0:HA], right, 13, -1),
    ]
    for c in flux_sends + table_sends + list_sends + mar_sends + air_sends:
        c.start()

    pairs = ab // 2 + SUB_A
    zero_block = jnp.zeros((BLOCK, BLOCK), BF16)

    def build_air(j, carry):
        op[j, 3 * BLOCK : 4 * BLOCK, 0:BLOCK] = zero_block
        op[j, 0:BLOCK, BLOCK : 2 * BLOCK] = zero_block
        for side in range(2):
            e = 2 * j + side
            b = lax.rem(e + ab - SUB_A, ab)
            links = lx[:, pl.ds(pl.multiple_of(e * BLOCK, BLOCK), BLOCK)] - b * BLOCK
            for part in range(3):
                ids = iota((BLOCK, BLOCK), 0) + part * BLOCK
                total = jnp.zeros((BLOCK, BLOCK), F32)
                for k in range(links.shape[0]):
                    total = total + jnp.where(links[k : k + 1, :] == ids, F32(1.0), F32(0.0))
                r = (part + side) * BLOCK
                op[j, r : r + BLOCK, side * BLOCK : (side + 1) * BLOCK] = total.astype(BF16)
        return carry

    lx[:, HA : HA + na] = alist[...]
    half = SUB_A // 2
    lax.fori_loop(half, pairs - half, build_air, 0)

    w_copy.wait()

    def split_weights(b, carry):
        hi, lo = pieces_of(wf[b])
        whi[b] = hi
        wlo[b] = lo
        return carry

    lax.fori_loop(0, ob, split_weights, 0)

    def place_of(b, r):
        ref = donor[r, me * ob + b]
        owner = ref // ab
        off = lax.rem(owner - me + n, n)
        base = jnp.where(off == 0, ab, jnp.where(off == 1, 2 * ab, 0))
        return base + lax.rem(ref, ab)

    for c in flux_sends:
        c.wait_recv()
    lane_ids = iota((8, BLOCK), 1)
    places = jnp.zeros((8, BLOCK), jnp.int32)
    for b in range(ob):
        picked = []
        for r in range(refs):
            where = place_of(b, r)
            places = jnp.where(lane_ids == b * refs + r, where, places)
            picked.append(cand[where])
        f = jnp.concatenate(picked, axis=1)
        hi = f.astype(BF16).astype(F32)
        stacked = jnp.concatenate([hi, f - hi], axis=0).astype(BF16)
        first = dot(stacked, whi[b])
        second = dot(stacked, wlo[b])
        ofx[FAR, :, b, :] = first[0:4] + first[4:8] + second[0:4]
    of_sends = [remote(ofx.at[FAR], ofx.at[FAR - d], 14 + i, d) for i, d in enumerate(far)]
    for c in of_sends:
        c.start()

    for c in table_sends:
        c.wait_recv()
    block_ids = iota((ob, BLOCK), 0) * BLOCK

    def prepare(s, carry):
        m = px[s, 12]
        total = jnp.zeros((ob, BLOCK), F32)
        for k in range(6):
            idx[s, k] = px[s, k].astype(jnp.int32) - block_ids
            w = px[s, 6 + k]
            total = total + w
            coef[s, k] = m * w
        coef[s, 6] = m * (1.0 - total)
        eta[pl.ds(pl.multiple_of(s * ob + 8, 8), ob), :] = m * px[s, 13]
        return carry

    slots = 2 * FAR + 1
    lax.fori_loop(0, slots, prepare, 0)
    eta[0:8, :] = jnp.zeros((8, BLOCK), F32)
    eta[8 + slots * ob : 16 + slots * ob, :] = jnp.zeros((8, BLOCK), F32)

    opairs = ob // 2 + BC_SUB

    def build_ocean(j, carry):
        for ref_ in (fhi, flo):
            ref_[j, 3 * BLOCK : 4 * BLOCK, 0:BLOCK] = zero_block
            ref_[j, 0:BLOCK, BLOCK : 2 * BLOCK] = zero_block
        for side in range(2):
            e = 2 * j + side + FAR * ob - BC_SUB
            s = e // ob
            b = lax.rem(e, ob)
            links = [idx[s, k, pl.ds(b, 1), :] for k in range(6)]
            values = [coef[s, k, pl.ds(b, 1), :] for k in range(7)]
            for part in range(3):
                ids = iota((BLOCK, BLOCK), 0) + part * BLOCK
                if part == 1:
                    own = iota((BLOCK, BLOCK), 0) == iota((BLOCK, BLOCK), 1)
                    total = jnp.where(own, values[6], F32(0.0))
                else:
                    total = jnp.zeros((BLOCK, BLOCK), F32)
                for k in range(6):
                    total = total + jnp.where(links[k] == ids, values[k], F32(0.0))
                r = (part + side) * BLOCK
                hi, lo = pieces_of(total)
                fhi[j, r : r + BLOCK, side * BLOCK : (side + 1) * BLOCK] = hi
                flo[j, r : r + BLOCK, side * BLOCK : (side + 1) * BLOCK] = lo
        return carry

    lax.fori_loop(0, opairs, build_ocean, 0)

    for c in of_sends:
        c.wait_recv()

    def neighbours(prev, cur, after, s):
        total = coef[s, 6] * cur
        for k in range(6):
            at = idx[s, k]
            lanes = jnp.bitwise_and(at, BLOCK - 1)
            g0 = gather_lanes(prev, lanes)
            g1 = gather_lanes(cur, lanes)
            g2 = gather_lanes(after, lanes)
            g = jnp.where(at < BLOCK, g0, jnp.where(at < 2 * BLOCK, g1, g2))
            total = total + coef[s, k] * g
        return total

    for s in range(slots):
        coef[s, 7] = 0.1 * ofx[s, 1] * px[s, 12]

    own_rows = slice(8 + FAR * ob, 8 + (FAR + 1) * ob)

    def barotropic(reach):
        def step(i, carry):
            fresh = []
            for s in range(FAR - reach, FAR + reach + 1):
                r = 8 + s * ob
                fresh.append(
                    coef[s, 7]
                    + neighbours(
                        eta[r - 1 : r - 1 + ob, :], eta[r : r + ob, :], eta[r + 1 : r + 1 + ob, :], s
                    )
                )
            for s, value in zip(range(FAR - reach, FAR + reach + 1), fresh):
                eta[8 + s * ob : 8 + (s + 1) * ob, :] = value
            return carry

        return step

    def eta_round(i):
        if i > 0:
            for c in eta_sends[-2:]:
                c.wait_recv()
            eta[8 : 8 + ob, :] = el[i - 1]
            eta[8 + (FAR + 1) * ob : 8 + (FAR + 2) * ob, :] = er[i - 1]
        lax.fori_loop(0, ROUNDS[i] - 1, barotropic(1), 0)
        barotropic(0)(0, 0)
        if i + 1 < len(ROUNDS):
            es[i] = eta[own_rows, :]
            pair = [
                remote(es.at[i], el.at[i], 22 + 2 * i, 1),
                remote(es.at[i], er.at[i], 23 + 2 * i, -1),
            ]
            for c in pair:
                c.start()
            eta_sends.extend(pair)
        else:
            ssh_out[...] = eta[own_rows, :]

    eta_sends = []
    eta_round(0)

    def put_ocean(value, at, buf):
        rows = value.reshape(rows_o, value.shape[2])
        hi, lo = pieces_of(rows)
        buf[0:rows_o, at : at + value.shape[2]] = hi
        buf[rows_o : 2 * rows_o, at : at + value.shape[2]] = lo

    edge_o = jnp.zeros((2 * rows_o, BLOCK), BF16)
    xa[:, 0:BLOCK] = edge_o
    xa[:, xa.shape[1] - BLOCK : xa.shape[1]] = edge_o
    mar_copy.wait()
    for b in range(ob):
        m = px[FAR, 12, b : b + 1, :]
        cols = slice(b * BLOCK, (b + 1) * BLOCK)
        put_ocean(xc[:, :, cols] * m, BLOCK + HO + b * BLOCK, xa)
    for c in mar_sends:
        c.wait_recv()
    for b in range(BC_SUB):
        cols = slice(b * BLOCK, (b + 1) * BLOCK)
        m = px[FAR - 1, 12, ob - BC_SUB + b : ob - BC_SUB + b + 1, :]
        put_ocean(xl[:, :, cols] * m, BLOCK + b * BLOCK, xa)
        m = px[FAR + 1, 12, b : b + 1, :]
        put_ocean(xr[:, :, cols] * m, BLOCK + HO + no + b * BLOCK, xa)

    def ocean_apply(j, src):
        window = src[:, pl.ds(pl.multiple_of(j * 2 * BLOCK, BLOCK), 4 * BLOCK)]
        a = dot(window, fhi[j])
        b = dot(window[0:rows_o], flo[j])
        return a[0:rows_o] + a[rows_o : 2 * rows_o] + b

    def ocean_first(j, carry):
        hi, lo = pieces_of(ocean_apply(j, xa))
        cols = pl.ds(pl.multiple_of(j * 2 * BLOCK + BLOCK, BLOCK), 2 * BLOCK)
        xb[0:rows_o, cols] = hi
        xb[rows_o : 2 * rows_o, cols] = lo
        return carry

    lax.fori_loop(0, opairs, ocean_first, 0)

    def ocean_second(j, carry):
        cols = pl.ds(pl.multiple_of((j - 1) * 2 * BLOCK, BLOCK), 2 * BLOCK)
        y_out[0:rows_o, cols] = ocean_apply(j, xb)
        return carry

    lax.fori_loop(1, opairs - 1, ocean_second, 0)

    gath[...] = jnp.zeros(gath.shape, F32)
    for i, field in enumerate((0, 2, 3)):
        for o in range(3):
            s = FAR - 1 + o
            forc[o * ob : (o + 1) * ob, :] = 0.2 * ofx[s, field] * px[s, 12]
        cur = forc[ob : 2 * ob, :]
        moved = neighbours(forc[ob - 1 : 2 * ob - 1, :], cur, forc[ob + 1 : 2 * ob + 1, :], FAR)
        gath[i] = moved
        gath[3 + i] = cur
    for b in range(ob):
        y_out[rows_o : rows_o + 16, b * BLOCK : (b + 1) * BLOCK] = gath[:, b, :]

    lo_op = level_operator(mdiff[...])
    l2 = dot_exact(lo_op[0:8], lo_op)
    width = y_out.shape[0]
    top = []
    cols = iota((1, width), 1)
    for f in range(3):
        n_l = levels_o
        place = (iota((n_l, width), 1) == iota((n_l, width), 0) + f * n_l).astype(F32)
        row = dot_exact(l2, place)[0:1]
        row = row + jnp.where(cols == rows_o + f, lo_op[0:1, 0:1], F32(0.0))
        top.append(row + jnp.where(cols == rows_o + 3 + f, F32(1.0), F32(0.0)))
    top = jnp.concatenate(top + [jnp.zeros((5, width), F32)], axis=0)
    thi = top.astype(BF16).astype(F32)
    tstack = jnp.concatenate([thi, top - thi], axis=0).astype(BF16)
    nt = (((1,), (1,)), ((), ()))
    for b in range(ob):
        yhi, ylo = pieces_of(y_out[:, b * BLOCK : (b + 1) * BLOCK])
        first = dot(tstack, yhi)
        second = dot(tstack, ylo)
        surf = first[0:8] + first[8:16] + second[0:8]
        row_ids = iota((8, BLOCK), 0)
        surf = jnp.where(row_ids == 3, px[FAR, 12, b : b + 1, :], surf)
        shi = surf.astype(BF16).astype(F32)
        sstack = jnp.concatenate([shi, surf - shi], axis=0).astype(BF16)
        first = lax.dot_general(sstack, whi[b], nt, preferred_element_type=F32)
        second = lax.dot_general(sstack, wlo[b], nt, preferred_element_type=F32)
        piece = first[0:8] + first[8:16] + second[0:8]
        for r in range(refs):
            pc[:, b * refs + r, :] = piece[0:4, r * BLOCK : (r + 1) * BLOCK]
    count = ob * refs
    hits = (iota((3 * ab, count), 0) == places[0:1, 0:count]).astype(F32)
    for f in range(4):
        coll[f] = dot_exact(hits, pc[f])
    back_sends = [
        remote(coll.at[:, 2 * ab : 3 * ab, :], rb.at[0], 20, 1),
        remote(coll.at[:, 0:ab, :], rb.at[1], 21, -1),
    ]
    for c in back_sends:
        c.start()

    eta_round(1)

    pad = jnp.zeros((rows_a - 3 * levels_a, 2 * BLOCK), F32)

    def put_air(value, at, buf):
        rows = jnp.concatenate([value.reshape(3 * levels_a, 2 * BLOCK), pad], axis=0)
        hi, lo = pieces_of(rows)
        buf[0:rows_a, at] = hi
        buf[rows_a : 2 * rows_a, at] = lo

    edge_a = jnp.zeros((2 * rows_a, BLOCK), BF16)
    for buf in (hla, hlb):
        buf[:, 0:BLOCK] = edge_a
        buf[:, buf.shape[1] - BLOCK : buf.shape[1]] = edge_a
    air_copy.wait()

    def fill(j, carry):
        cols = pl.ds(pl.multiple_of(j * 2 * BLOCK, BLOCK), 2 * BLOCK)
        put_air(
            centre[:, :, cols],
            pl.ds(pl.multiple_of(j * 2 * BLOCK + BLOCK + HA, BLOCK), 2 * BLOCK),
            hla,
        )
        return carry

    lax.fori_loop(0, ab // 2, fill, 0)
    def air_apply(j, src):
        window = src[:, pl.ds(pl.multiple_of(j * 2 * BLOCK, BLOCK), 4 * BLOCK)]
        r = dot(window, op[j])
        own = src[:, pl.ds(pl.multiple_of(j * 2 * BLOCK + BLOCK, BLOCK), 2 * BLOCK)].astype(F32)
        own = own[0:rows_a] + own[rows_a : 2 * rows_a]
        gain = 1.0 - 0.22 * alist.shape[0]
        return gain * own + 0.22 * (r[0:rows_a] + r[rows_a : 2 * rows_a])

    def air_step(src, dst):
        def step(j, carry):
            hi, lo = pieces_of(air_apply(j, src))
            cols = pl.ds(pl.multiple_of(j * 2 * BLOCK + BLOCK, BLOCK), 2 * BLOCK)
            dst[0:rows_a, cols] = hi
            dst[rows_a : 2 * rows_a, cols] = lo
            return carry

        return step

    inner = half + 1
    lax.fori_loop(inner, pairs - inner, air_step(hla, hlb), 0)
    lax.fori_loop(inner + 1, pairs - inner - 1, air_step(hlb, hla), 0)
    eta_round(2)

    for c in list_sends + air_sends:
        c.wait_recv()
    lx[:, 0:HA] = lleft[...]
    lx[:, HA + na : 2 * HA + na] = lright[...]
    lax.fori_loop(0, half, build_air, 0)
    lax.fori_loop(pairs - half, pairs, build_air, 0)
    for j in range(half):
        cols = slice(j * 2 * BLOCK, (j + 1) * 2 * BLOCK)
        base = BLOCK + j * 2 * BLOCK
        put_air(left[:, :, cols], slice(base, base + 2 * BLOCK), hla)
        base = base + HA + na
        put_air(right[:, :, cols], slice(base, base + 2 * BLOCK), hla)

    lax.fori_loop(0, inner, air_step(hla, hlb), 0)
    lax.fori_loop(pairs - inner, pairs, air_step(hla, hlb), 0)
    lax.fori_loop(1, inner + 1, air_step(hlb, hla), 0)
    lax.fori_loop(pairs - inner - 1, pairs - 1, air_step(hlb, hla), 0)
    lax.fori_loop(1, pairs - 1, air_step(hla, hlb), 0)

    def air_last(j, carry):
        cols = pl.ds(pl.multiple_of((j - half) * 2 * BLOCK, BLOCK), 2 * BLOCK)
        t_out[:, cols] = air_apply(j, hlb)
        return carry

    lax.fori_loop(half, pairs - half, air_last, 0)

    for c in back_sends:
        c.wait_recv()
    tot_out[...] = coll[:, ab : 2 * ab, :] + rb[0] + rb[1]
    for c in flux_sends + table_sends + list_sends + mar_sends + air_sends + of_sends + back_sends + eta_sends:
        c.wait_send()


def last_kernel(
    t_in, y_in, tot_in, ssh_in, warm_in, adiff_in, mdiff_in,
    a_out, o_out, skin, ssh_out,
    t, y, tot, warm, adiff, mdiff,
    mix_a, mix_o, a_buf, o_buf, sem, in_sem,
):
    moves = [(adiff_in, adiff), (mdiff_in, mdiff), (t_in, t), (y_in, y), (tot_in, tot), (warm_in, warm), (ssh_in, ssh_out)]
    ins = [pltpu.make_async_copy(a, b, in_sem.at[i]) for i, (a, b) in enumerate(moves)]
    for c in ins:
        c.start()
    ins[0].wait()
    ins[1].wait()
    rows_a = t.shape[0]
    rows_o = y.shape[0]
    la = adiff.shape[0]
    lo = mdiff.shape[0]
    one = level_operator(adiff[...])
    two = dot_exact(one, one)
    four = dot_exact(two, two)
    oc = level_operator(mdiff[...])
    oc2 = dot_exact(oc, oc)
    at = iota((lo, rows_o), 1)
    level = iota((lo, rows_o), 0)
    for f in range(3):
        m = spread_columns(four, f, rows_a)
        mix_a[f * la : (f + 1) * la, :] = m
        m = spread_columns(oc2, f, rows_o)
        m = m + jnp.where(at == 3 * lo + f, oc[:, 0:1], F32(0.0))
        m = m + jnp.where((at == 3 * lo + 3 + f) & (level == 0), F32(1.0), F32(0.0))
        mix_o[f * lo : (f + 1) * lo, :] = m

    def mix(src, mixer, buf, out, levels):
        mhi, mlo = pieces_of(mixer[...])

        for j in range(src.shape[1] // (2 * BLOCK)):
            cols = slice(j * 2 * BLOCK, (j + 1) * 2 * BLOCK)
            hi, lo_ = pieces_of(src[:, cols])
            r = dot(mhi, hi) + dot(mlo, hi) + dot(mhi, lo_)
            buf[:, :, cols] = r.reshape(3, levels, 2 * BLOCK)
            copy = pltpu.make_async_copy(buf.at[:, :, cols], out.at[:, :, cols], sem.at[len(copies)])
            copy.start()
            copies.append(copy)

    copies = []
    ins[2].wait()
    mix(t, mix_a, a_buf, a_out, la)
    ins[3].wait()
    mix(y, mix_o, o_buf, o_out, lo)
    for c in ins[4:]:
        c.wait()
    share = 1.0 + tot[3]
    parts = [(warm[...] + tot[0]) / share, tot[1] / share, tot[2] / share]
    for f in range(3):
        for b in range(tot.shape[1]):
            skin[f : f + 1, b * BLOCK : (b + 1) * BLOCK] = parts[f][b : b + 1, :]
    for copy in copies:
        copy.wait()


def body(
    air, warm, alist, adiff, mar, sea, mlist, mff, mind, mdiff, donor, weights
):
    n = lax.axis_size("col")
    na = air.shape[2]
    no = mar.shape[2]
    ab = na // BLOCK
    ob = no // BLOCK
    la = air.shape[1]
    lo = mar.shape[1]
    refs = donor.shape[1]
    rows_a = -(-3 * la // 16) * 16
    rows_o = 3 * lo
    slots = 2 * FAR + 1
    pairs = ab // 2 + SUB_A
    opairs = ob // 2 + BC_SUB
    wide_a = na + 2 * HA + 2 * BLOCK
    wide_o = no + 2 * HO + 2 * BLOCK
    vmem = pl.BlockSpec(memory_space=pltpu.VMEM)
    hbm = pl.BlockSpec(memory_space=pl.ANY)
    S = jax.ShapeDtypeStruct
    V = pltpu.VMEM
    t, y, tot, ssh = pl.pallas_call(
        functools.partial(main_kernel, n),
        out_shape=(
            S((rows_a, na), F32), S((rows_o + 16, no), F32), S((4, ab, BLOCK), F32), S((ob, BLOCK), F32),
        ),
        in_specs=[hbm] * 11,
        out_specs=(vmem, vmem, vmem, vmem),
        scratch_shapes=[
            V((1, na), F32), V(alist.shape, jnp.int32), V((ob, BLOCK), F32), V(mlist.shape, jnp.int32),
            V(mff.shape, F32), V((ob, BLOCK), jnp.int32), V(mdiff.shape, F32),
            pltpu.SMEM((refs, donor.shape[0]), jnp.int32),
            V((3, 8, na), F32),
            V((3, la, na), F32), V((3, la, HA), F32), V((3, la, HA), F32),
            V((3, lo, no), F32), V((3, lo, HO), F32), V((3, lo, HO), F32),
            V((4, na + 2 * HA), jnp.int32), V((4, HA), jnp.int32), V((4, HA), jnp.int32),
            V((ob, refs * BLOCK, BLOCK), F32),
            V((ob, refs * BLOCK, BLOCK), BF16), V((ob, refs * BLOCK, BLOCK), BF16),
            V((3 * ab, 4, BLOCK), F32),
            V((slots, 14, ob, BLOCK), F32),
            V((slots, 4, ob, BLOCK), F32),
            V((slots, 6, ob, BLOCK), jnp.int32), V((slots, 8, ob, BLOCK), F32),
            V((slots * ob + 16, BLOCK), F32),
            V((3 * ob, BLOCK), F32),
            V((16, ob, BLOCK), F32),
            V((pairs, 4 * BLOCK, 2 * BLOCK), BF16),
            V((opairs, 4 * BLOCK, 2 * BLOCK), BF16), V((opairs, 4 * BLOCK, 2 * BLOCK), BF16),
            V((2 * rows_a, wide_a), BF16), V((2 * rows_a, wide_a), BF16),
            V((2 * rows_o, wide_o), BF16), V((2 * rows_o, wide_o), BF16),
            V((4, ob * refs, BLOCK), F32), V((4, 3 * ab, BLOCK), F32), V((2, 4, ab, BLOCK), F32),
            V((2, ob, BLOCK), F32), V((2, ob, BLOCK), F32), V((2, ob, BLOCK), F32),
            pltpu.SemaphoreType.DMA((26,)), pltpu.SemaphoreType.DMA((26,)), pltpu.SemaphoreType.DMA((12,)),
        ],
        compiler_params=pltpu.CompilerParams(
            collective_id=0, has_side_effects=True, vmem_limit_bytes=63 * 1024 * 1024
        ),
        name="couple",
    )(
        air, warm.reshape(1, na), alist, mar, sea.reshape(ob, BLOCK), mlist, mff,
        mind.reshape(ob, BLOCK), mdiff, donor.T, weights.reshape(ob, refs * BLOCK, BLOCK),
    )
    a_out, o_out, skin, ssh_out = pl.pallas_call(
        last_kernel,
        out_shape=(S(air.shape, F32), S(mar.shape, F32), S((3, na), F32), S((ob, BLOCK), F32)),
        in_specs=[hbm] * 7,
        out_specs=(hbm, hbm, vmem, vmem),
        scratch_shapes=[
            V((rows_a, na), F32), V((rows_o + 16, no), F32), V((4, ab, BLOCK), F32), V((ab, BLOCK), F32),
            V(adiff.shape, F32), V(mdiff.shape, F32),
            V((3 * la, rows_a), F32), V((3 * lo, rows_o + 16), F32), V(air.shape, F32), V(mar.shape, F32),
            pltpu.SemaphoreType.DMA(((na + no) // (2 * BLOCK),)),
            pltpu.SemaphoreType.DMA((7,)),
        ],
        compiler_params=pltpu.CompilerParams(vmem_limit_bytes=63 * 1024 * 1024),
        name="mix",
    )(t, y, tot, ssh, warm.reshape(ab, BLOCK), adiff, mdiff)
    return a_out, o_out, ssh_out.reshape(no), skin


def solution(mesh):
    cells = ("member", "col")
    in_specs = (
        P(None, None, cells),
        P(cells),
        P(None, "col"),
        P(),
        P(None, None, cells),
        P(cells),
        P(None, "col"),
        P(None, "col"),
        P("col"),
        P(),
        P(),
        P("col", None, None, None),
    )
    out_specs = (P(None, None, cells), P(None, None, cells), P(cells), P(None, cells))
    return jax.shard_map(body, mesh=mesh, in_specs=in_specs, out_specs=out_specs, check_vma=False)
```

```python
import functools

import jax
import jax.numpy as jnp
from jax import lax
from jax.experimental import pallas as pl
from jax.experimental.pallas import tpu as pltpu
from jax.sharding import PartitionSpec as P

BLOCK = 128
SUB_A = 4
BT_SUB = 10
BC_SUB = 2
MESH = pl.DeviceIdType.MESH
F32 = jnp.float32
BF16 = jnp.bfloat16
HIGHEST = lax.Precision.HIGHEST
FAR = 1
ROUNDS = (7, 7, 6)
HA = SUB_A * BLOCK
HO = BC_SUB * BLOCK


def iota(shape, dim):
    return lax.broadcasted_iota(jnp.int32, shape, dim)


def dot(a, b):
    return jnp.dot(a, b, preferred_element_type=F32)


def dot_exact(a, b):
    return jnp.dot(a, b, preferred_element_type=F32, precision=HIGHEST)


def pieces_of(x):
    hi = x.astype(BF16)
    return hi, (x - hi.astype(F32)).astype(BF16)


def level_operator(profile):
    n = profile.shape[0]
    return profile + jnp.where(iota((n, n), 0) == iota((n, n), 1), F32(0.6), F32(0.0))


def spread_columns(matrix, field, width):
    n = matrix.shape[0]
    place = (iota((n, width), 1) == iota((n, width), 0) + field * n).astype(F32)
    return dot_exact(matrix, place)


def gather_lanes(rows, lanes):
    return jnp.take_along_axis(rows, lanes, axis=1, mode="promise_in_bounds")


def main_kernel(
    n,
    air, warm_in, alist_in, mar, sea_in, mlist_in, mff_in, mind_in, mdiff_in, donor_in, weights,
    t_out, y_out, tot_out, ssh_out,
    warm, alist, sea, mlist, mff, mind, mdiff, donor,
    low, centre, left, right, xc, xl, xr, lx, lleft, lright,
    wf, whi, wlo, cand, px, ofx, idx, coef, eta, forc, gath, op, fhi, flo,
    hla, hlb, xa, xb, pc, coll, rb, es, el, er,
    ss, rs, ls,
):
    levels_a = air.shape[1]
    levels_o = mar.shape[1]
    na = air.shape[2]
    no = mar.shape[2]
    ab = na // BLOCK
    ob = no // BLOCK
    rows_a = hla.shape[0] // 2
    rows_o = xa.shape[0] // 2
    refs = donor_in.shape[0]
    me = lax.axis_index("col")

    def peer(d):
        return {"col": lax.rem(me + d + n, n)}

    def remote(src, dst, i, d):
        return pltpu.make_async_remote_copy(
            src_ref=src, dst_ref=dst, send_sem=ss.at[i], recv_sem=rs.at[i],
            device_id=peer(d), device_id_type=MESH,
        )

    low_copy = pltpu.make_async_copy(air.at[:, levels_a - 8 :, :], low, ls.at[0])
    low_copy.start()
    small = [
        pltpu.make_async_copy(a, b, ls.at[4 + i])
        for i, (a, b) in enumerate(
            [
                (mlist_in, mlist), (mff_in, mff), (mind_in, mind), (sea_in, sea),
                (warm_in, warm), (alist_in, alist), (donor_in, donor), (mdiff_in, mdiff),
            ]
        )
    ]
    for c in small:
        c.start()
    w_copy = pltpu.make_async_copy(weights, wf, ls.at[1])
    air_copy = pltpu.make_async_copy(air, centre, ls.at[2])
    mar_copy = pltpu.make_async_copy(mar, xc, ls.at[3])
    w_copy.start()
    mar_copy.start()
    air_copy.start()
    far = [d for d in range(-FAR, FAR + 1) if d != 0]
    barrier = pltpu.get_barrier_semaphore()
    for d in far:
        pl.semaphore_signal(barrier, inc=1, device_id=peer(d), device_id_type=MESH)

    for c in small:
        c.wait()

    for b in range(ob):
        cols = slice(b * BLOCK, (b + 1) * BLOCK)
        px[FAR, 0:6, b, :] = mlist[:, cols].astype(F32)
        px[FAR, 6:12, b, :] = mff[:, cols]
    px[FAR, 12, :, :] = mind[...].astype(F32)
    px[FAR, 13, :, :] = sea[...]

    low_copy.wait()
    lowest = [low[f, 7:8, :] for f in range(3)]
    flux = jnp.concatenate(
        [
            0.5 * (lowest[0] - warm[...]),
            0.3 * lowest[1] * lowest[2],
            0.5 * lowest[1],
            0.5 * lowest[2],
        ],
        axis=0,
    )
    for b in range(ab):
        cand[ab + b] = flux[:, b * BLOCK : (b + 1) * BLOCK]

    pl.semaphore_wait(barrier, len(far))
    flux_sends = [
        remote(cand.at[ab : 2 * ab], cand.at[0:ab], 0, 1),
        remote(cand.at[ab : 2 * ab], cand.at[2 * ab : 3 * ab], 1, -1),
    ]
    table_sends = [remote(px.at[FAR], px.at[FAR - d], 2 + i, d) for i, d in enumerate(far)]
    list_sends = [
        remote(alist.at[:, na - HA : na], lleft, 8, 1),
        remote(alist.at[:, 0:HA], lright, 9, -1),
    ]
    mar_sends = [
        remote(mar.at[:, :, no - HO : no], xl, 10, 1),
        remote(mar.at[:, :, 0:HO], xr, 11, -1),
    ]
    air_sends = [
        remote(air.at[:, :, na - HA : na], left, 12, 1),
        remote(air.at[:, :, 0:HA], right, 13, -1),
    ]
    for c in flux_sends + table_sends + list_sends + mar_sends + air_sends:
        c.start()

    pairs = ab // 2 + SUB_A
    zero_block = jnp.zeros((BLOCK, BLOCK), BF16)

    def build_air(j, carry):
        op[j, 3 * BLOCK : 4 * BLOCK, 0:BLOCK] = zero_block
        op[j, 0:BLOCK, BLOCK : 2 * BLOCK] = zero_block
        for side in range(2):
            e = 2 * j + side
            b = lax.rem(e + ab - SUB_A, ab)
            links = lx[:, pl.ds(pl.multiple_of(e * BLOCK, BLOCK), BLOCK)] - b * BLOCK
            for part in range(3):
                ids = iota((BLOCK, BLOCK), 0) + part * BLOCK
                total = jnp.zeros((BLOCK, BLOCK), F32)
                for k in range(links.shape[0]):
                    total = total + jnp.where(links[k : k + 1, :] == ids, F32(1.0), F32(0.0))
                r = (part + side) * BLOCK
                op[j, r : r + BLOCK, side * BLOCK : (side + 1) * BLOCK] = total.astype(BF16)
        return carry

    lx[:, HA : HA + na] = alist[...]
    half = SUB_A // 2
    lax.fori_loop(half, pairs - half, build_air, 0)

    w_copy.wait()

    def split_weights(b, carry):
        hi, lo = pieces_of(wf[b])
        whi[b] = hi
        wlo[b] = lo
        return carry

    lax.fori_loop(0, ob, split_weights, 0)

    def place_of(b, r):
        at = donor[r, me * ob + b] - (me - 1) * ab
        at = jnp.where(at < 0, at + n * ab, at)
        at = jnp.where(at >= n * ab, at - n * ab, at)
        return jnp.minimum(jnp.maximum(at, 0), 3 * ab - 1)

    for c in flux_sends:
        c.wait_recv()
    lane_ids = iota((8, BLOCK), 1)
    places = jnp.zeros((8, BLOCK), jnp.int32)
    for b in range(ob):
        picked = []
        for r in range(refs):
            where = place_of(b, r)
            places = jnp.where(lane_ids == b * refs + r, where, places)
            picked.append(cand[where])
        f = jnp.concatenate(picked, axis=1)
        hi = f.astype(BF16).astype(F32)
        stacked = jnp.concatenate([hi, f - hi], axis=0).astype(BF16)
        first = dot(stacked, whi[b])
        second = dot(stacked, wlo[b])
        ofx[FAR, :, b, :] = first[0:4] + first[4:8] + second[0:4]
    of_sends = [remote(ofx.at[FAR], ofx.at[FAR - d], 14 + i, d) for i, d in enumerate(far)]
    for c in of_sends:
        c.start()

    for c in table_sends:
        c.wait_recv()
    block_ids = iota((ob, BLOCK), 0) * BLOCK

    def prepare(s, carry):
        m = px[s, 12]
        total = jnp.zeros((ob, BLOCK), F32)
        for k in range(6):
            idx[s, k] = px[s, k].astype(jnp.int32) - block_ids
            w = px[s, 6 + k]
            total = total + w
            coef[s, k] = m * w
        coef[s, 6] = m * (1.0 - total)
        eta[pl.ds(pl.multiple_of(s * ob + 8, 8), ob), :] = m * px[s, 13]
        return carry

    slots = 2 * FAR + 1
    lax.fori_loop(0, slots, prepare, 0)
    eta[0:8, :] = jnp.zeros((8, BLOCK), F32)
    eta[8 + slots * ob : 16 + slots * ob, :] = jnp.zeros((8, BLOCK), F32)

    opairs = ob // 2 + BC_SUB

    def build_ocean(j, carry):
        for ref_ in (fhi, flo):
            ref_[j, 3 * BLOCK : 4 * BLOCK, 0:BLOCK] = zero_block
            ref_[j, 0:BLOCK, BLOCK : 2 * BLOCK] = zero_block
        for side in range(2):
            e = 2 * j + side + FAR * ob - BC_SUB
            s = e // ob
            b = lax.rem(e, ob)
            links = [idx[s, k, pl.ds(b, 1), :] for k in range(6)]
            values = [coef[s, k, pl.ds(b, 1), :] for k in range(7)]
            for part in range(3):
                ids = iota((BLOCK, BLOCK), 0) + part * BLOCK
                if part == 1:
                    own = iota((BLOCK, BLOCK), 0) == iota((BLOCK, BLOCK), 1)
                    total = jnp.where(own, values[6], F32(0.0))
                else:
                    total = jnp.zeros((BLOCK, BLOCK), F32)
                for k in range(6):
                    total = total + jnp.where(links[k] == ids, values[k], F32(0.0))
                r = (part + side) * BLOCK
                hi, lo = pieces_of(total)
                fhi[j, r : r + BLOCK, side * BLOCK : (side + 1) * BLOCK] = hi
                flo[j, r : r + BLOCK, side * BLOCK : (side + 1) * BLOCK] = lo
        return carry

    lax.fori_loop(0, opairs, build_ocean, 0)

    pad = jnp.zeros((rows_a - 3 * levels_a, 2 * BLOCK), F32)

    def put_air(value, at, buf):
        rows = jnp.concatenate([value.reshape(3 * levels_a, 2 * BLOCK), pad], axis=0)
        hi, lo = pieces_of(rows)
        buf[0:rows_a, at] = hi
        buf[rows_a : 2 * rows_a, at] = lo

    edge_a = jnp.zeros((2 * rows_a, BLOCK), BF16)
    for buf in (hla, hlb):
        buf[:, 0:BLOCK] = edge_a
        buf[:, buf.shape[1] - BLOCK : buf.shape[1]] = edge_a
    air_copy.wait()

    def fill(j, carry):
        cols = pl.ds(pl.multiple_of(j * 2 * BLOCK, BLOCK), 2 * BLOCK)
        put_air(
            centre[:, :, cols],
            pl.ds(pl.multiple_of(j * 2 * BLOCK + BLOCK + HA, BLOCK), 2 * BLOCK),
            hla,
        )
        return carry

    lax.fori_loop(0, ab // 2, fill, 0)
    def air_apply(j, src):
        window = src[:, pl.ds(pl.multiple_of(j * 2 * BLOCK, BLOCK), 4 * BLOCK)]
        r = dot(window, op[j])
        own = src[:, pl.ds(pl.multiple_of(j * 2 * BLOCK + BLOCK, BLOCK), 2 * BLOCK)].astype(F32)
        own = own[0:rows_a] + own[rows_a : 2 * rows_a]
        gain = 1.0 - 0.22 * alist.shape[0]
        return gain * own + 0.22 * (r[0:rows_a] + r[rows_a : 2 * rows_a])

    def air_step(src, dst):
        def step(j, carry):
            hi, lo = pieces_of(air_apply(j, src))
            cols = pl.ds(pl.multiple_of(j * 2 * BLOCK + BLOCK, BLOCK), 2 * BLOCK)
            dst[0:rows_a, cols] = hi
            dst[rows_a : 2 * rows_a, cols] = lo
            return carry

        return step

    inner = half + 1
    lax.fori_loop(inner, pairs - inner, air_step(hla, hlb), 0, unroll=2)
    lax.fori_loop(inner + 1, pairs - inner - 1, air_step(hlb, hla), 0, unroll=2)

    for c in of_sends:
        c.wait_recv()

    def neighbours(prev, cur, after, s):
        total = coef[s, 6] * cur
        for k in range(6):
            at = idx[s, k]
            lanes = jnp.bitwise_and(at, BLOCK - 1)
            g0 = gather_lanes(prev, lanes)
            g1 = gather_lanes(cur, lanes)
            g2 = gather_lanes(after, lanes)
            g = jnp.where(at < BLOCK, g0, jnp.where(at < 2 * BLOCK, g1, g2))
            total = total + coef[s, k] * g
        return total

    for s in range(slots):
        coef[s, 7] = 0.1 * ofx[s, 1] * px[s, 12]

    own_rows = slice(8 + FAR * ob, 8 + (FAR + 1) * ob)

    def barotropic(reach):
        def step(i, carry):
            fresh = []
            for s in range(FAR - reach, FAR + reach + 1):
                r = 8 + s * ob
                fresh.append(
                    coef[s, 7]
                    + neighbours(
                        eta[r - 1 : r - 1 + ob, :], eta[r : r + ob, :], eta[r + 1 : r + 1 + ob, :], s
                    )
                )
            for s, value in zip(range(FAR - reach, FAR + reach + 1), fresh):
                eta[8 + s * ob : 8 + (s + 1) * ob, :] = value
            return carry

        return step

    def eta_round(i):
        if i > 0:
            for c in eta_sends[-2:]:
                c.wait_recv()
            eta[8 : 8 + ob, :] = el[i - 1]
            eta[8 + (FAR + 1) * ob : 8 + (FAR + 2) * ob, :] = er[i - 1]
        lax.fori_loop(0, ROUNDS[i] - 1, barotropic(1), 0)
        barotropic(0)(0, 0)
        if i + 1 < len(ROUNDS):
            es[i] = eta[own_rows, :]
            pair = [
                remote(es.at[i], el.at[i], 22 + 2 * i, 1),
                remote(es.at[i], er.at[i], 23 + 2 * i, -1),
            ]
            for c in pair:
                c.start()
            eta_sends.extend(pair)
        else:
            ssh_out[...] = eta[own_rows, :]

    eta_sends = []
    eta_round(0)

    def put_ocean(value, at, buf):
        rows = value.reshape(rows_o, value.shape[2])
        hi, lo = pieces_of(rows)
        buf[0:rows_o, at : at + value.shape[2]] = hi
        buf[rows_o : 2 * rows_o, at : at + value.shape[2]] = lo

    edge_o = jnp.zeros((2 * rows_o, BLOCK), BF16)
    xa[:, 0:BLOCK] = edge_o
    xa[:, xa.shape[1] - BLOCK : xa.shape[1]] = edge_o
    mar_copy.wait()
    for b in range(ob):
        m = px[FAR, 12, b : b + 1, :]
        cols = slice(b * BLOCK, (b + 1) * BLOCK)
        put_ocean(xc[:, :, cols] * m, BLOCK + HO + b * BLOCK, xa)
    for c in mar_sends:
        c.wait_recv()
    for b in range(BC_SUB):
        cols = slice(b * BLOCK, (b + 1) * BLOCK)
        m = px[FAR - 1, 12, ob - BC_SUB + b : ob - BC_SUB + b + 1, :]
        put_ocean(xl[:, :, cols] * m, BLOCK + b * BLOCK, xa)
        m = px[FAR + 1, 12, b : b + 1, :]
        put_ocean(xr[:, :, cols] * m, BLOCK + HO + no + b * BLOCK, xa)

    def ocean_apply(j, src):
        window = src[:, pl.ds(pl.multiple_of(j * 2 * BLOCK, BLOCK), 4 * BLOCK)]
        a = dot(window, fhi[j])
        b = dot(window[0:rows_o], flo[j])
        return a[0:rows_o] + a[rows_o : 2 * rows_o] + b

    def ocean_first(j, carry):
        hi, lo = pieces_of(ocean_apply(j, xa))
        cols = pl.ds(pl.multiple_of(j * 2 * BLOCK + BLOCK, BLOCK), 2 * BLOCK)
        xb[0:rows_o, cols] = hi
        xb[rows_o : 2 * rows_o, cols] = lo
        return carry

    lax.fori_loop(0, opairs, ocean_first, 0)

    def ocean_second(j, carry):
        cols = pl.ds(pl.multiple_of((j - 1) * 2 * BLOCK, BLOCK), 2 * BLOCK)
        y_out[0:rows_o, cols] = ocean_apply(j, xb)
        return carry

    lax.fori_loop(1, opairs - 1, ocean_second, 0)

    gath[...] = jnp.zeros(gath.shape, F32)
    for i, field in enumerate((0, 2, 3)):
        for o in range(3):
            s = FAR - 1 + o
            forc[o * ob : (o + 1) * ob, :] = 0.2 * ofx[s, field] * px[s, 12]
        cur = forc[ob : 2 * ob, :]
        moved = neighbours(forc[ob - 1 : 2 * ob - 1, :], cur, forc[ob + 1 : 2 * ob + 1, :], FAR)
        gath[i] = moved
        gath[3 + i] = cur
    for b in range(ob):
        y_out[rows_o : rows_o + 16, b * BLOCK : (b + 1) * BLOCK] = gath[:, b, :]

    lo_op = level_operator(mdiff[...])
    l2 = dot_exact(lo_op[0:8], lo_op)
    width = y_out.shape[0]
    top = []
    cols = iota((1, width), 1)
    for f in range(3):
        n_l = levels_o
        place = (iota((n_l, width), 1) == iota((n_l, width), 0) + f * n_l).astype(F32)
        row = dot_exact(l2, place)[0:1]
        row = row + jnp.where(cols == rows_o + f, lo_op[0:1, 0:1], F32(0.0))
        top.append(row + jnp.where(cols == rows_o + 3 + f, F32(1.0), F32(0.0)))
    top = jnp.concatenate(top + [jnp.zeros((5, width), F32)], axis=0)
    thi = top.astype(BF16).astype(F32)
    tstack = jnp.concatenate([thi, top - thi], axis=0).astype(BF16)
    nt = (((1,), (1,)), ((), ()))
    for b in range(ob):
        yhi, ylo = pieces_of(y_out[:, b * BLOCK : (b + 1) * BLOCK])
        first = dot(tstack, yhi)
        second = dot(tstack, ylo)
        surf = first[0:8] + first[8:16] + second[0:8]
        row_ids = iota((8, BLOCK), 0)
        surf = jnp.where(row_ids == 3, px[FAR, 12, b : b + 1, :], surf)
        shi = surf.astype(BF16).astype(F32)
        sstack = jnp.concatenate([shi, surf - shi], axis=0).astype(BF16)
        first = lax.dot_general(sstack, whi[b], nt, preferred_element_type=F32)
        second = lax.dot_general(sstack, wlo[b], nt, preferred_element_type=F32)
        piece = first[0:8] + first[8:16] + second[0:8]
        for r in range(refs):
            pc[:, b * refs + r, :] = piece[0:4, r * BLOCK : (r + 1) * BLOCK]
    count = ob * refs
    hits = (iota((3 * ab, count), 0) == places[0:1, 0:count]).astype(F32)
    for f in range(4):
        coll[f] = dot_exact(hits, pc[f])
    back_sends = [
        remote(coll.at[:, 2 * ab : 3 * ab, :], rb.at[0], 20, 1),
        remote(coll.at[:, 0:ab, :], rb.at[1], 21, -1),
    ]
    for c in back_sends:
        c.start()

    eta_round(1)

    for c in list_sends + air_sends:
        c.wait_recv()
    lx[:, 0:HA] = lleft[...]
    lx[:, HA + na : 2 * HA + na] = lright[...]
    lax.fori_loop(0, half, build_air, 0)
    lax.fori_loop(pairs - half, pairs, build_air, 0)
    for j in range(half):
        cols = slice(j * 2 * BLOCK, (j + 1) * 2 * BLOCK)
        base = BLOCK + j * 2 * BLOCK
        put_air(left[:, :, cols], slice(base, base + 2 * BLOCK), hla)
        base = base + HA + na
        put_air(right[:, :, cols], slice(base, base + 2 * BLOCK), hla)

    lax.fori_loop(0, inner, air_step(hla, hlb), 0, unroll=2)
    lax.fori_loop(pairs - inner, pairs, air_step(hla, hlb), 0, unroll=2)
    lax.fori_loop(1, inner + 1, air_step(hlb, hla), 0, unroll=2)
    lax.fori_loop(pairs - inner - 1, pairs - 1, air_step(hlb, hla), 0, unroll=2)
    eta_round(2)
    lax.fori_loop(1, pairs - 1, air_step(hla, hlb), 0, unroll=2)

    def air_last(j, carry):
        cols = pl.ds(pl.multiple_of((j - half) * 2 * BLOCK, BLOCK), 2 * BLOCK)
        t_out[:, cols] = air_apply(j, hlb)
        return carry

    lax.fori_loop(half, pairs - half, air_last, 0, unroll=2)

    for c in back_sends:
        c.wait_recv()
    tot_out[...] = coll[:, ab : 2 * ab, :] + rb[0] + rb[1]
    for c in flux_sends + table_sends + list_sends + mar_sends + air_sends + of_sends + back_sends + eta_sends:
        c.wait_send()


def last_kernel(
    t_in, y_in, tot_in, ssh_in, warm_in, adiff_in, mdiff_in,
    a_out, o_out, skin, ssh_out,
    t, y, tot, warm, adiff, mdiff,
    mix_a, mix_o, a_buf, o_buf, sem, in_sem,
):
    moves = [(adiff_in, adiff), (mdiff_in, mdiff), (t_in, t), (y_in, y), (tot_in, tot), (warm_in, warm), (ssh_in, ssh_out)]
    ins = [pltpu.make_async_copy(a, b, in_sem.at[i]) for i, (a, b) in enumerate(moves)]
    for c in ins:
        c.start()
    ins[0].wait()
    ins[1].wait()
    rows_a = t.shape[0]
    rows_o = y.shape[0]
    la = adiff.shape[0]
    lo = mdiff.shape[0]
    one = level_operator(adiff[...])
    two = dot_exact(one, one)
    four = dot_exact(two, two)
    oc = level_operator(mdiff[...])
    oc2 = dot_exact(oc, oc)
    at = iota((lo, rows_o), 1)
    level = iota((lo, rows_o), 0)
    for f in range(3):
        m = spread_columns(four, f, rows_a)
        mix_a[f * la : (f + 1) * la, :] = m
        m = spread_columns(oc2, f, rows_o)
        m = m + jnp.where(at == 3 * lo + f, oc[:, 0:1], F32(0.0))
        m = m + jnp.where((at == 3 * lo + 3 + f) & (level == 0), F32(1.0), F32(0.0))
        mix_o[f * lo : (f + 1) * lo, :] = m

    def mix(src, mixer, buf, out, levels):
        mhi, mlo = pieces_of(mixer[...])

        for j in range(src.shape[1] // (2 * BLOCK)):
            cols = slice(j * 2 * BLOCK, (j + 1) * 2 * BLOCK)
            hi, lo_ = pieces_of(src[:, cols])
            r = dot(mhi, hi) + dot(mlo, hi) + dot(mhi, lo_)
            buf[:, :, cols] = r.reshape(3, levels, 2 * BLOCK)
            copy = pltpu.make_async_copy(buf.at[:, :, cols], out.at[:, :, cols], sem.at[len(copies)])
            copy.start()
            copies.append(copy)

    copies = []
    ins[2].wait()
    mix(t, mix_a, a_buf, a_out, la)
    ins[3].wait()
    mix(y, mix_o, o_buf, o_out, lo)
    for c in ins[4:]:
        c.wait()
    share = 1.0 + tot[3]
    parts = [(warm[...] + tot[0]) / share, tot[1] / share, tot[2] / share]
    for f in range(3):
        for b in range(tot.shape[1]):
            skin[f : f + 1, b * BLOCK : (b + 1) * BLOCK] = parts[f][b : b + 1, :]
    for copy in copies:
        copy.wait()


def body(
    air, warm, alist, adiff, mar, sea, mlist, mff, mind, mdiff, donor, weights
):
    n = lax.axis_size("col")
    na = air.shape[2]
    no = mar.shape[2]
    ab = na // BLOCK
    ob = no // BLOCK
    la = air.shape[1]
    lo = mar.shape[1]
    refs = donor.shape[1]
    rows_a = -(-3 * la // 16) * 16
    rows_o = 3 * lo
    slots = 2 * FAR + 1
    pairs = ab // 2 + SUB_A
    opairs = ob // 2 + BC_SUB
    wide_a = na + 2 * HA + 2 * BLOCK
    wide_o = no + 2 * HO + 2 * BLOCK
    vmem = pl.BlockSpec(memory_space=pltpu.VMEM)
    hbm = pl.BlockSpec(memory_space=pl.ANY)
    S = jax.ShapeDtypeStruct
    V = pltpu.VMEM
    t, y, tot, ssh = pl.pallas_call(
        functools.partial(main_kernel, n),
        out_shape=(
            S((rows_a, na), F32), S((rows_o + 16, no), F32), S((4, ab, BLOCK), F32), S((ob, BLOCK), F32),
        ),
        in_specs=[hbm] * 11,
        out_specs=(vmem, vmem, vmem, vmem),
        scratch_shapes=[
            V((1, na), F32), V(alist.shape, jnp.int32), V((ob, BLOCK), F32), V(mlist.shape, jnp.int32),
            V(mff.shape, F32), V((ob, BLOCK), jnp.int32), V(mdiff.shape, F32),
            pltpu.SMEM((refs, donor.shape[0]), jnp.int32),
            V((3, 8, na), F32),
            V((3, la, na), F32), V((3, la, HA), F32), V((3, la, HA), F32),
            V((3, lo, no), F32), V((3, lo, HO), F32), V((3, lo, HO), F32),
            V((4, na + 2 * HA), jnp.int32), V((4, HA), jnp.int32), V((4, HA), jnp.int32),
            V((ob, refs * BLOCK, BLOCK), F32),
            V((ob, refs * BLOCK, BLOCK), BF16), V((ob, refs * BLOCK, BLOCK), BF16),
            V((3 * ab, 4, BLOCK), F32),
            V((slots, 14, ob, BLOCK), F32),
            V((slots, 4, ob, BLOCK), F32),
            V((slots, 6, ob, BLOCK), jnp.int32), V((slots, 8, ob, BLOCK), F32),
            V((slots * ob + 16, BLOCK), F32),
            V((3 * ob, BLOCK), F32),
            V((16, ob, BLOCK), F32),
            V((pairs, 4 * BLOCK, 2 * BLOCK), BF16),
            V((opairs, 4 * BLOCK, 2 * BLOCK), BF16), V((opairs, 4 * BLOCK, 2 * BLOCK), BF16),
            V((2 * rows_a, wide_a), BF16), V((2 * rows_a, wide_a), BF16),
            V((2 * rows_o, wide_o), BF16), V((2 * rows_o, wide_o), BF16),
            V((4, ob * refs, BLOCK), F32), V((4, 3 * ab, BLOCK), F32), V((2, 4, ab, BLOCK), F32),
            V((2, ob, BLOCK), F32), V((2, ob, BLOCK), F32), V((2, ob, BLOCK), F32),
            pltpu.SemaphoreType.DMA((26,)), pltpu.SemaphoreType.DMA((26,)), pltpu.SemaphoreType.DMA((12,)),
        ],
        compiler_params=pltpu.CompilerParams(
            collective_id=0, has_side_effects=True, vmem_limit_bytes=63 * 1024 * 1024
        ),
        name="couple",
    )(
        air, warm.reshape(1, na), alist, mar, sea.reshape(ob, BLOCK), mlist, mff,
        mind.reshape(ob, BLOCK), mdiff, donor.T, weights.reshape(ob, refs * BLOCK, BLOCK),
    )
    a_out, o_out, skin, ssh_out = pl.pallas_call(
        last_kernel,
        out_shape=(S(air.shape, F32), S(mar.shape, F32), S((3, na), F32), S((ob, BLOCK), F32)),
        in_specs=[hbm] * 7,
        out_specs=(hbm, hbm, vmem, vmem),
        scratch_shapes=[
            V((rows_a, na), F32), V((rows_o + 16, no), F32), V((4, ab, BLOCK), F32), V((ab, BLOCK), F32),
            V(adiff.shape, F32), V(mdiff.shape, F32),
            V((3 * la, rows_a), F32), V((3 * lo, rows_o + 16), F32), V(air.shape, F32), V(mar.shape, F32),
            pltpu.SemaphoreType.DMA(((na + no) // (2 * BLOCK),)),
            pltpu.SemaphoreType.DMA((7,)),
        ],
        compiler_params=pltpu.CompilerParams(vmem_limit_bytes=63 * 1024 * 1024),
        name="mix",
    )(t, y, tot, ssh, warm.reshape(ab, BLOCK), adiff, mdiff)
    return a_out, o_out, ssh_out.reshape(no), skin


def solution(mesh):
    cells = ("member", "col")
    in_specs = (
        P(None, None, cells),
        P(cells),
        P(None, "col"),
        P(),
        P(None, None, cells),
        P(cells),
        P(None, "col"),
        P(None, "col"),
        P("col"),
        P(),
        P(),
        P("col", None, None, None),
    )
    out_specs = (P(None, None, cells), P(None, None, cells), P(cells), P(None, cells))
    return jax.shard_map(body, mesh=mesh, in_specs=in_specs, out_specs=out_specs, check_vma=False)
```
